32 devices in a mesh: head: 4 (over y, core), ctx: 8 (over z, x).
Axes of the slice: x: 2, y: 2, z: 4, core: 2. Of those that a mesh axis runs over, the one named last changes fastest.
Arguments:
- query_matrix: bfloat16 [4096, 4096], P(('ctx', 'head')), may hold values from -6 to 6
- key_matrix: bfloat16 [4096, 2048], P(('ctx', 'head')), may hold values from -6 to 6
- value_matrix: bfloat16 [4096, 2048], P(('ctx', 'head')), may hold values from -6 to 6
- documents: int32 [4096], replicated, may hold values from 0 to 6, as said below
- readers: int32 [8, 4], replicated, may hold values from 0 to 1, as said below
Outputs:
- attended: bfloat16 [4096, 4096], P(('ctx', 'head'))
The draws below stay inside these ranges and needn't reach their ends.
Inputs may be any that keep to these rules, and one draw needn't show every extreme that they name: `documents`: starts at 0 and never falls from one token to the next; it rises by one exactly twice inside every key block other than key blocks 0 to 3 and 0 to 4, and nowhere else. `readers`: every entry of column 0 is 1. Row 0 and rows 0 to 4 are all 1.
All inputs are finite; a program needn't handle non-finite values.
Results may differ from the reference program's by a relative error of at most 0.0038.
Values may be sent and summed in bfloat16 or wider, within the bound.
No kernel may reach another device: no remote copies, remote signals or barrier semaphores. Data moves between devices by JAX's collectives and lax.ppermute only.
A program may use at most 192 MiB of HBM per device.

```python
import jax
import jax.numpy as jnp
from jax import lax

QUERY_HEADS = 32
KEY_VALUE_HEADS = 16
HEAD_WIDTH = 128
TOK_DEV = 128
WIN = 4
BLOCK = 512
KEY_BLOCK_COUNT = 8
PACKED_TOKENS = 4096
N_HEAD = 4


def states_pair(key):
    base = jax.random.fold_in(key, 7)
    query_key, key_random_seed = jax.random.split(base, 2)
    query_matrix_local = jax.random.truncated_normal(query_key, -6.0, 6.0, (PACKED_TOKENS, QUERY_HEADS * HEAD_WIDTH), jnp.float32)
    sampled_keys = jax.random.truncated_normal(key_random_seed, -6.0, 6.0, (PACKED_TOKENS, KEY_VALUE_HEADS * HEAD_WIDTH), jnp.float32)
    return (query_matrix_local, sampled_keys)


def draw_query_matrix(key, part):
    return states_pair(key)[0].astype(jnp.bfloat16)


def draw_key_matrix(key, part):
    return states_pair(key)[1].astype(jnp.bfloat16)


def forced_rows(block_ids):
    middle = KEY_BLOCK_COUNT // 2
    lowest = max(middle - WIN, 0)
    return (block_ids == 0) | (block_ids >= lowest) & (block_ids <= middle)


def draw_documents(key, part):
    first_key, second_key = jax.random.split(jax.random.fold_in(key, 23))
    half_block = BLOCK // 2
    first_offset = jax.random.randint(first_key, (KEY_BLOCK_COUNT,), 1, half_block)
    second_offset = jax.random.randint(second_key, (KEY_BLOCK_COUNT,), half_block, BLOCK)
    positions = jnp.arange(PACKED_TOKENS, dtype=jnp.int32)
    block_ids = positions // BLOCK
    offsets = positions % BLOCK
    middle = KEY_BLOCK_COUNT // 2
    lowest = max(middle - WIN, 0)
    kept_whole = (block_ids < WIN) | (block_ids >= lowest) & (block_ids <= middle)
    starts = (offsets == first_offset[block_ids]) | (offsets == second_offset[block_ids])
    starts = starts & jnp.logical_not(kept_whole)
    return jnp.cumsum(starts.astype(jnp.int32)).astype(jnp.int32)


def draw_readers(key, part):
    level_key, pick_key = jax.random.split(jax.random.fold_in(key, 11))
    levels = jax.random.randint(level_key, (KEY_BLOCK_COUNT, 1), 0, 5)
    picks = jax.random.randint(pick_key, (KEY_BLOCK_COUNT, WIN), 0, 4)
    column = jnp.arange(WIN)[None, :]
    full_rows = forced_rows(jnp.arange(KEY_BLOCK_COUNT, dtype=jnp.int32))[:, None]
    return jnp.where((column == 0) | (picks < levels) | full_rows, 1, 0).astype(jnp.int32)


def steps_of(stream_key, dims, pieces, least, high):
    gain, own = 1.0, jax.random.fold_in(stream_key, 6)
    for dim, blocks in pieces:
        steps = jnp.exp(jax.random.uniform(jax.random.fold_in(own, dim), (blocks,), jnp.float32, least / len(pieces), high / len(pieces)))
        gain = gain * jnp.repeat(steps, dims[dim] // blocks).reshape([-1 if axis == dim else 1 for axis in range(len(dims))])
    return gain


def normal_values(rng, shape, spread, bound, cuts=(), held_as=jnp.bfloat16):
    values = jax.random.normal(rng, shape, jnp.float32) * spread
    if len(cuts) > 0:
        values = steps_of(rng, shape, cuts, -0.22, 0.18) * values
    return jnp.clip(values, min=-bound, max=bound).astype(held_as)


def setup_inputs(seed: int = 0) -> dict:
    streams_of = jax.random.split(jax.random.key(seed), 6)
    return {
        "query_matrix": draw_query_matrix(jax.random.fold_in(streams_of[5], 71), 0),
        "key_matrix": draw_key_matrix(jax.random.fold_in(streams_of[5], 71), 0),
        "value_matrix": normal_values(streams_of[2], (PACKED_TOKENS, KEY_VALUE_HEADS * HEAD_WIDTH), 1.0, 6.0, ((0, 32),)),
        "documents": draw_documents(jax.random.fold_in(streams_of[5], 71), 0),
        "readers": draw_readers(jax.random.fold_in(streams_of[5], 71), 0),
    }


score_scale = 168.0 ** -0.5
neg_large = -1.0e30


def reference(query_matrix, key_matrix, value_matrix, documents, readers):
    rows_per_block = TOK_DEV * N_HEAD
    query_group_width = QUERY_HEADS // KEY_VALUE_HEADS
    padding_length = (WIN - 1) * rows_per_block
    query_matrix_local = query_matrix.astype(jnp.float32).reshape(KEY_BLOCK_COUNT, rows_per_block, KEY_VALUE_HEADS, query_group_width, HEAD_WIDTH)
    key_matrix_padded = jnp.concatenate([jnp.zeros((padding_length, KEY_VALUE_HEADS * HEAD_WIDTH), jnp.float32), key_matrix.astype(jnp.float32)], axis=0).reshape(-1, KEY_VALUE_HEADS, HEAD_WIDTH)
    value_matrix_padded = jnp.concatenate([jnp.zeros((padding_length, KEY_VALUE_HEADS * HEAD_WIDTH), jnp.float32), value_matrix.astype(jnp.float32)], axis=0).reshape(-1, KEY_VALUE_HEADS, HEAD_WIDTH)
    padded_docs = jnp.concatenate([jnp.full((padding_length,), -1, jnp.int32), documents.astype(jnp.int32)], axis=0)

    def one_block(block_index):
        block_index = block_index.astype(jnp.int32)
        query_block = lax.dynamic_index_in_dim(query_matrix_local, block_index, 0, False)
        start = (block_index * rows_per_block).astype(jnp.int32)
        key_block = lax.dynamic_slice_in_dim(key_matrix_padded, start, WIN * rows_per_block, 0)
        value_block = lax.dynamic_slice_in_dim(value_matrix_padded, start, WIN * rows_per_block, 0)
        key_docs = lax.dynamic_slice_in_dim(padded_docs, start, WIN * rows_per_block, 0)
        query_docs = lax.dynamic_slice_in_dim(documents.astype(jnp.int32), start, rows_per_block, 0)
        key_pos = (block_index - WIN + 1) * rows_per_block + jnp.arange(WIN * rows_per_block, dtype=jnp.int32)
        query_pos = start + jnp.arange(rows_per_block, dtype=jnp.int32)
        owners = block_index - WIN + 1 + jnp.arange(WIN, dtype=jnp.int32)
        distances = WIN - 1 - jnp.arange(WIN, dtype=jnp.int32)
        permitted = (owners >= 0) & (readers[jnp.maximum(owners, 0), distances] > 0)
        permitted_keys = jnp.repeat(permitted, rows_per_block)
        visible = (query_docs[:, None] == key_docs[None, :]) & (key_pos[None, :] <= query_pos[:, None]) & permitted_keys[None, :]

        def one_head(operands):
            query_head, key_head, value_head = operands
            scores = jnp.einsum("qmd,kd->qmk", query_head, key_head) * score_scale
            scores = jnp.where(visible[:, None, :], scores, neg_large)
            row_max = jnp.max(scores, axis=2, keepdims=True)
            weights = jnp.where(visible[:, None, :], jnp.exp(scores - row_max), 0.0)
            totals = jnp.sum(weights, axis=2)
            rounded = lax.optimization_barrier(weights.astype(jnp.bfloat16))
            mixture = jnp.einsum("qmk,kd->qmd", rounded.astype(jnp.float32), value_head)
            return mixture / totals[..., None]

        head_outputs = lax.map(one_head, (jnp.moveaxis(query_block, 1, 0), jnp.moveaxis(key_block, 1, 0), jnp.moveaxis(value_block, 1, 0)))
        return jnp.moveaxis(head_outputs, 0, 1).reshape(rows_per_block, QUERY_HEADS * HEAD_WIDTH).astype(jnp.bfloat16)

    result = lax.map(one_block, jnp.arange(KEY_BLOCK_COUNT, dtype=jnp.int32))
    return result.reshape(PACKED_TOKENS, QUERY_HEADS * HEAD_WIDTH)
```

```python
import functools
import math

import jax
import jax.numpy as jnp
from jax import lax
from jax.experimental import pallas as pl
from jax.experimental.pallas import tpu as pltpu
from jax.sharding import PartitionSpec as P

QUERY_HEADS = 32
KEY_VALUE_HEADS = 16
HEAD_WIDTH = 128
GROUP = QUERY_HEADS // KEY_VALUE_HEADS

log_scale = 168.0 ** (-0.5) * math.log2(math.e)
neg_large = -1e30
VMEM_LIMIT = 40 * 1024 * 1024


def wanted_blocks(count, window):
    middle = count // 2
    whole = set(range(window)) | set(range(max(middle - window, 0), middle + 1))
    return [
        [b for b in range(max(0, t - window + 1), t) if all(m in whole for m in range(b + 1, t))]
        for t in range(count)
    ]


def plan_rounds(count, window, kind, early):
    wanted = wanted_blocks(count, window)
    held = [{c: 0} for c in range(count)]
    rounds = []

    def missing(t):
        return [b for b in wanted[t] if b not in held[t]]

    def send(k, s, t, b):
        rounds[k][t] = (s, b, held[s][b])
        held[t][b] = k + 1

    for k in range(3):
        rounds.append({})
        had = [dict(x) for x in held]
        for s in range(count):
            t = s + 2 if (k + kind) % 2 == 0 else s ^ 1
            if t >= count:
                continue
            choice = [b for b in had[s] if b in missing(t)]
            if choice:
                send(k, s, t, max(choice))
    for t in range(count):
        for b in missing(t):
            whole_way = t - b == 1 or early
            placed = False
            if whole_way:
                for k in range(len(rounds)):
                    busy = {entry[0] for entry in rounds[k].values()}
                    if b not in busy and t not in rounds[k]:
                        send(k, b, t, b)
                        placed = True
                        break
            k = 3
            while not placed:
                if k == len(rounds):
                    rounds.append({})
                busy = {entry[0] for entry in rounds[k].values()}
                holders = [
                    s
                    for s in range(count)
                    if b in held[s] and held[s][b] <= k and s not in busy
                ]
                holders.sort(key=lambda s: (abs(t - s) != 2, abs(t - s)))
                if holders and t not in rounds[k]:
                    send(k, holders[0], t, b)
                    placed = True
                k += 1
    return rounds


def move(operands, copies, shapes, head_index):
    count_in = len(operands)

    def kernel(head_ref, *refs):
        h = head_ref[0]
        sources, targets, sems = refs[:count_in], refs[count_in:-1], refs[-1]

        def at(value):
            return pl.multiple_of(value(h), 128) if callable(value) else value

        started = []
        for number, (s, row, rows, col, cols, t, to_row, to_col) in enumerate(copies):
            copy = pltpu.make_async_copy(
                sources[s].at[pl.ds(at(row), rows), pl.ds(at(col), cols)],
                targets[t].at[pl.ds(at(to_row), rows), pl.ds(at(to_col), cols)],
                sems.at[number],
            )
            copy.start()
            started.append(copy)
        for copy in started:
            copy.wait()

    moved = sum(c[2] * c[4] * 2 for c in copies)
    return pl.pallas_call(
        kernel,
        out_shape=[jax.ShapeDtypeStruct(s, jnp.bfloat16) for s in shapes],
        grid_spec=pltpu.PrefetchScalarGridSpec(
            num_scalar_prefetch=1,
            grid=(1,),
            in_specs=[pl.BlockSpec(memory_space=pl.ANY)] * count_in,
            out_specs=[pl.BlockSpec(memory_space=pl.ANY)] * len(shapes),
            scratch_shapes=[pltpu.SemaphoreType.DMA((len(copies),))],
        ),
        cost_estimate=pl.CostEstimate(flops=0, bytes_accessed=2 * moved, transcendentals=0),
    )(head_index, *operands)


def attend(queries, chunk, blocks, with_own, state, final, meta, documents, doc_rows, readers, window):
    slots = len(queries)
    token_count = queries[0].shape[0]
    rows = slots * token_count
    kv_heads = blocks[0].shape[1] // (2 * HEAD_WIDTH)
    width = GROUP * HEAD_WIDTH
    count = len(blocks)

    def kernel(meta_ref, doc_ref, read_ref, *refs):
        refs = list(refs)
        q_refs = [refs.pop(0) for _ in range(slots)]
        kv_refs = [(refs.pop(0), refs.pop(0)) for _ in range(count)]
        rows_ref = refs.pop(0)
        if not with_own:
            acc_in, stat_in = refs.pop(0), refs.pop(0)
        if final:
            out_refs = [refs.pop(0) for _ in range(slots)]
        else:
            acc_out, stat_out = refs.pop(0), refs.pop(0)
        q_all, acc, top, total, bias = refs
        step = pl.program_id(0)
        ctx, head = meta_ref[0], meta_ref[1]

        for r in range(slots):
            q_all[r * token_count : (r + 1) * token_count, :] = q_refs[r][...]
        if not with_own:
            acc[...] = acc_in[...]
            for g in range(GROUP):
                stats = stat_in[:, g * HEAD_WIDTH : (g + 1) * HEAD_WIDTH]
                top[g] = stats[:, 0:1]
                total[g] = stats[:, HEAD_WIDTH // 2 : HEAD_WIDTH // 2 + 1]

        def make_bias(index, block, own):
            def of_queries(i, _):
                place_q = head ^ i
                here = rows_ref[pl.ds(ctx * slots + place_q, 1), :]
                q_docs = jnp.broadcast_to(here, (token_count, token_count)).T
                for j in range(slots):
                    place_k = head ^ j
                    k_docs = rows_ref[pl.ds(block * slots + place_k, 1), :]
                    seen = q_docs == k_docs
                    if own:
                        q_pos = place_q * token_count + lax.broadcasted_iota(
                            jnp.int32, (token_count, token_count), 0
                        )
                        k_pos = place_k * token_count + lax.broadcasted_iota(
                            jnp.int32, (token_count, token_count), 1
                        )
                        seen = seen & (k_pos <= q_pos)
                    bias[
                        index,
                        pl.ds(pl.multiple_of(i * token_count, token_count), token_count),
                        j * token_count : (j + 1) * token_count,
                    ] = jnp.where(seen, 0.0, neg_large)
                return 0

            lax.fori_loop(0, slots, of_queries, 0)

        def run(index, masked, first):
            k_ref, v_ref = kv_refs[index]

            def tile(i, _):
                part = pl.ds(pl.multiple_of(i * token_count, token_count), token_count)
                for g in range(GROUP):
                    lanes = slice(g * HEAD_WIDTH, (g + 1) * HEAD_WIDTH)
                    scores = lax.dot_general(
                        q_all[part, lanes],
                        k_ref[...],
                        (((1,), (1,)), ((), ())),
                        preferred_element_type=jnp.float32,
                    )
                    if masked:
                        scores = scores + bias[index, part, :]
                    peak = jnp.max(scores, axis=1, keepdims=True)
                    if not first:
                        before = top[g, part, :]
                        peak = jnp.maximum(peak, before)
                    weights = jnp.exp2((scores - peak) * log_scale)
                    product = jnp.dot(
                        weights.astype(jnp.bfloat16),
                        v_ref[...],
                        preferred_element_type=jnp.float32,
                    )
                    added = jnp.sum(weights, axis=1, keepdims=True)
                    if first:
                        total[g, part, :] = added
                        acc[part, lanes] = product
                    else:
                        fade = jnp.exp2((before - peak) * log_scale)
                        total[g, part, :] = total[g, part, :] * fade + added
                        acc[part, lanes] = acc[part, lanes] * fade + product
                    top[g, part, :] = peak
                return 0

            lax.fori_loop(0, slots, tile, 0, unroll=2)

        q_first, q_last = doc_ref[ctx * rows], doc_ref[ctx * rows + rows - 1]
        other = 0
        for index in range(count):
            if with_own and index == 0:

                @pl.when(step == 0)
                def _():
                    make_bias(0, ctx, True)

                run(0, True, True)
                continue
            number = meta_ref[2 + other]
            other += 1
            block = jnp.maximum(number, 0)
            k_first, k_last = doc_ref[block * rows], doc_ref[block * rows + rows - 1]
            distance = jnp.clip(ctx - block, 0, window - 1)
            live = (
                (number >= 0) & (read_ref[block * window + distance] > 0) & (k_last == q_first)
            )
            full = k_first == q_last

            @pl.when(live & full)
            def _(index=index):
                run(index, False, False)

            @pl.when(live & jnp.logical_not(full))
            def _(index=index, block=block):
                @pl.when(step == 0)
                def _():
                    make_bias(index, block, False)

                run(index, True, False)

        if final:
            for r in range(slots):
                part = slice(r * token_count, (r + 1) * token_count)
                for g in range(GROUP):
                    lanes = slice(g * HEAD_WIDTH, (g + 1) * HEAD_WIDTH)
                    out_refs[r][:, lanes] = (acc[part, lanes] / total[g, part, :]).astype(
                        jnp.bfloat16
                    )
        else:
            acc_out[...] = acc[...]
            low = lax.broadcasted_iota(jnp.int32, (rows, HEAD_WIDTH), 1) < HEAD_WIDTH // 2
            for g in range(GROUP):
                stat_out[:, g * HEAD_WIDTH : (g + 1) * HEAD_WIDTH] = jnp.where(
                    low, top[g], total[g]
                )

    kv_specs = []
    kv_operands = []
    for block in blocks:
        kv_specs.append(pl.BlockSpec((rows, HEAD_WIDTH), lambda i, *_: (0, i)))
        kv_specs.append(pl.BlockSpec((rows, HEAD_WIDTH), lambda i, *_: (0, i + kv_heads)))
        kv_operands += [block, block]
    wide = pl.BlockSpec((rows, width), lambda i, *_: (0, i))
    thin = pl.BlockSpec((token_count, width), lambda i, *_: (0, i))
    in_specs = [
        pl.BlockSpec((token_count, width), lambda i, *_: (0, i + chunk * kv_heads))
        for _ in range(slots)
    ]
    in_specs += kv_specs + [pl.BlockSpec(doc_rows.shape, lambda i, *_: (0, 0))]
    operands = list(queries) + kv_operands + [doc_rows]
    if not with_own:
        in_specs += [wide, wide]
        operands += list(state)
    if final:
        out_shape = [jax.ShapeDtypeStruct((token_count, kv_heads * width), jnp.bfloat16)] * slots
        out_specs = [thin] * slots
    else:
        out_shape = [jax.ShapeDtypeStruct((rows, kv_heads * width), jnp.float32)] * 2
        out_specs = [wide, wide]
    scores_made = kv_heads * GROUP * rows * rows * count
    return pl.pallas_call(
        kernel,
        out_shape=out_shape,
        grid_spec=pltpu.PrefetchScalarGridSpec(
            num_scalar_prefetch=3,
            grid=(kv_heads,),
            in_specs=in_specs,
            out_specs=out_specs,
            scratch_shapes=[
                pltpu.VMEM((rows, width), jnp.bfloat16),
                pltpu.VMEM((rows, width), jnp.float32),
                pltpu.VMEM((GROUP, rows, 1), jnp.float32),
                pltpu.VMEM((GROUP, rows, 1), jnp.float32),
                pltpu.VMEM((count, rows, rows), jnp.float32),
            ],
        ),
        compiler_params=pltpu.CompilerParams(vmem_limit_bytes=VMEM_LIMIT),
        cost_estimate=pl.CostEstimate(
            flops=4 * scores_made * HEAD_WIDTH,
            bytes_accessed=4 * rows * kv_heads * width,
            transcendentals=scores_made,
        ),
    )(meta, documents, readers, *operands)


def per_device(query_matrix, key_matrix, value_matrix, documents, readers):
    shards = lax.axis_size("ctx")
    slots = lax.axis_size("head")
    window = readers.shape[1]
    tokens = query_matrix.shape[0]
    rows = tokens * slots
    heads_local = key_matrix.shape[1] // HEAD_WIDTH // slots
    chunks = 2 if heads_local % 2 == 0 else 1
    chunk_heads = heads_local // chunks
    chunk_keys = chunk_heads * HEAD_WIDTH
    chunk_queries = chunk_keys * GROUP
    ctx, head = lax.axis_index("ctx"), lax.axis_index("head")
    head_index = head.astype(jnp.int32).reshape(1)
    doc_rows = documents.reshape(shards * slots, tokens)

    plans = []
    for chunk in range(chunks):
        kinds = [plan_rounds(shards, window, kind, chunk == chunks - 1) for kind in (0, 1)]
        length = max(len(k) for k in kinds)
        plans.append([k + [{}] * (length - len(k)) for k in kinds])
    table = [
        [
            [
                value
                for plan in plans
                for k in range(len(plan[0]))
                for value in (
                    next((e[2] for e in plan[h % 2][k].values() if e[0] == c), -1),
                    plan[h % 2][k][c][1] if c in plan[h % 2][k] else -1,
                )
            ]
            for h in range(slots)
        ]
        for c in range(shards)
    ]
    mine = lax.dynamic_slice(
        jnp.array(table, jnp.int32), (ctx, head, 0), (1, 1, len(table[0][0]))
    ).reshape(-1)

    def swap(value, r):
        return lax.ppermute(value, "head", [(h, h ^ r) for h in range(slots)])

    copies = []
    shapes = []
    for chunk in range(chunks):
        for r in range(slots):
            for source in range(2):
                copies.append(
                    (
                        source,
                        0,
                        tokens,
                        lambda h, r=r, chunk=chunk: (h ^ r) * (heads_local * HEAD_WIDTH)
                        + chunk * chunk_keys,
                        chunk_keys,
                        chunk * slots + r,
                        0,
                        source * chunk_keys,
                    )
                )
            shapes.append((tokens, 2 * chunk_keys))
    pieces = move([key_matrix, value_matrix], copies, shapes, head_index)
    own = []
    for chunk in range(chunks):
        parts = pieces[chunk * slots : (chunk + 1) * slots]
        parts = [parts[0]] + [swap(parts[r], r) for r in range(1, slots)]
        own.append(
            move(
                parts,
                [(r, 0, tokens, 0, 2 * chunk_keys, 0, r * tokens, 0) for r in range(slots)],
                [(rows, 2 * chunk_keys)],
                head_index,
            )[0]
        )
    local_queries = GROUP * heads_local * HEAD_WIDTH
    queries = move(
        [query_matrix],
        [
            (0, 0, tokens, lambda h, r=r: (h ^ r) * local_queries, local_queries, r, 0, 0)
            for r in range(slots)
        ],
        [(tokens, local_queries)] * slots,
        head_index,
    )
    queries = [queries[0]] + [swap(queries[r], r) for r in range(1, slots)]

    held = [[block] for block in own]
    numbers = [[] for _ in own]
    cursor = [sum(2 * len(plans[p][0]) for p in range(chunk)) for chunk in range(chunks)]
    for k in range(max(len(plan[0]) for plan in plans)):
        for chunk in range(chunks):
            kinds = plans[chunk]
            if k >= len(kinds[0]):
                continue
            pairs, used = [], set()
            for h in range(slots):
                for target, (source, _, slot) in kinds[h % 2][k].items():
                    pairs.append((h * shards + source, h * shards + target))
                    used.add(slot)
            used = sorted(used)
            operand = held[chunk][used[0]]
            for slot in used[1:]:
                operand = jnp.where(
                    mine[cursor[chunk] + 2 * k] == slot, held[chunk][slot], operand
                )
            numbers[chunk].append(mine[cursor[chunk] + 2 * k + 1])
            held[chunk].append(lax.ppermute(operand, ("head", "ctx"), pairs))

    results = []
    for chunk in range(chunks):
        blocks, ids = held[chunk], numbers[chunk]
        place = jnp.stack([ctx, head]).astype(jnp.int32)
        common = (documents, doc_rows, readers.reshape(-1), window)
        state = attend(
            queries, chunk, blocks[:3], True, None, False,
            jnp.concatenate([place, jnp.stack(ids[:2])]), *common,
        )
        outs = attend(
            queries, chunk, blocks[3:], False, state, True,
            jnp.concatenate([place, jnp.stack(ids[2:])]), *common,
        )
        results += [outs[0]] + [swap(outs[r], r) for r in range(1, slots)]

    return move(
        results,
        [
            (
                chunk * slots + r,
                0,
                tokens,
                0,
                chunk_queries,
                0,
                0,
                lambda h, r=r, chunk=chunk: (h ^ r) * local_queries + chunk * chunk_queries,
            )
            for chunk in range(chunks)
            for r in range(slots)
        ],
        [query_matrix.shape],
        head_index,
    )[0]


def solution(mesh):
    placed = (
        P(("ctx", "head"), None),
        P(("ctx", "head"), None),
        P(("ctx", "head"), None),
        P(),
        P(),
    )
    return jax.shard_map(
        per_device, mesh=mesh, in_specs=placed, out_specs=P(("ctx", "head"), None), check_vma=False
    )
```

```python
import functools
import math

import jax
import jax.numpy as jnp
from jax import lax
from jax.experimental import pallas as pl
from jax.experimental.pallas import tpu as pltpu
from jax.sharding import PartitionSpec as P

QUERY_HEADS = 32
KEY_VALUE_HEADS = 16
HEAD_WIDTH = 128
GROUP = QUERY_HEADS // KEY_VALUE_HEADS

log_scale = 168.0 ** (-0.5) * math.log2(math.e)
neg_large = -1e30
SMALL_VMEM = 4 * 1024 * 1024


def wanted_blocks(count, window):
    middle = count // 2
    whole = set(range(window)) | set(range(max(middle - window, 0), middle + 1))
    return [
        [b for b in range(max(0, t - window + 1), t) if all(m in whole for m in range(b + 1, t))]
        for t in range(count)
    ]


def plan_rounds(count, window, kind, direct):
    wanted = wanted_blocks(count, window)
    held = [{c: 0} for c in range(count)]
    rounds = []

    def missing(t):
        return [b for b in wanted[t] if b not in held[t]]

    def send(k, s, t, b):
        rounds[k][t] = (s, b, held[s][b])
        held[t][b] = k + 1

    def free(k, s, t):
        return t not in rounds[k] and all(entry[0] != s for entry in rounds[k].values())

    for k in range(3):
        rounds.append({})
        had = [dict(x) for x in held]
        for s in range(count):
            t = s + 2 if (k + kind) % 2 == 0 else s ^ 1
            if t >= count:
                continue
            choice = [b for b in had[s] if b in missing(t)]
            if choice:
                send(k, s, t, max(choice))
    for t in range(count):
        for b in missing(t):
            options = [
                (k, b) for k in range(3) if t - b == 1 and (k + kind) % 2 == 0 and free(k, b, t)
            ]
            k = 3
            while not options:
                if k == len(rounds):
                    rounds.append({})
                holders = [s for s in range(count) if held[s].get(b, k + 1) <= k and free(k, s, t)]
                if direct:
                    holders = [s for s in holders if s == b]
                holders.sort(key=lambda s: (abs(t - s) != 2, abs(t - s)))
                options = [(k, s) for s in holders]
                k += 1
            send(options[0][0], options[0][1], t, b)
    return rounds


in_smem = pl.BlockSpec(memory_space=pltpu.SMEM)
in_vmem = pl.BlockSpec(memory_space=pltpu.VMEM)
anywhere = pl.BlockSpec(memory_space=pl.ANY)
in_hbm = pl.BlockSpec(memory_space=pltpu.HBM)


def move(place, operands, copies, shapes, source_spec, target_spec, after=(), weight=1):
    count_in = len(operands)

    def kernel(place_ref, *refs):
        h = place_ref[1]
        sources, targets, sems = refs[:count_in], refs[count_in + len(after) : -1], refs[-1]

        def span(value, size):
            return pl.ds(pl.multiple_of(value(h), 128) if callable(value) else value, size)

        started = []
        for number, (s, row, rows, col, cols, t, to_row, to_col) in enumerate(copies):
            copy = pltpu.make_async_copy(
                sources[s].at[span(row, rows), span(col, cols)],
                targets[t].at[span(to_row, rows), span(to_col, cols)],
                sems.at[number],
            )
            copy.start()
            started.append(copy)
        for copy in started:
            copy.wait()

    return pl.pallas_call(
        kernel,
        out_shape=[jax.ShapeDtypeStruct(s, jnp.bfloat16) for s in shapes],
        in_specs=[in_smem] + [source_spec] * count_in + [anywhere] * len(after),
        out_specs=[target_spec] * len(shapes),
        scratch_shapes=[pltpu.SemaphoreType.DMA((len(copies),))],
        compiler_params=pltpu.CompilerParams(
            vmem_limit_bytes=SMALL_VMEM
        ),
        cost_estimate=pl.CostEstimate(
            flops=0,
            bytes_accessed=weight * sum(4 * c[2] * c[4] for c in copies),
            transcendentals=0,
        ),
    )(place, *operands, *after)


def survey(place, table, documents, readers, entries, rounds, window, slots, rows):
    def kernel(place_ref, table_ref, doc_ref, read_ref, out_ref):
        ctx, head = place_ref[0], place_ref[1]
        out_ref[0] = ctx
        out_ref[1] = head
        base = (ctx * slots + head) * entries
        q_first, q_last = doc_ref[ctx * rows], doc_ref[ctx * rows + rows - 1]
        for k in range(rounds):
            number = table_ref[base + k]
            block = jnp.maximum(number, 0)
            k_first, k_last = doc_ref[block * rows], doc_ref[block * rows + rows - 1]
            distance = jnp.clip(ctx - block, 0, window - 1)
            live = (
                (number >= 0) & (read_ref[block * window + distance] > 0) & (k_last == q_first)
            )
            out_ref[2 + 3 * k] = block
            out_ref[3 + 3 * k] = live.astype(jnp.int32)
            out_ref[4 + 3 * k] = (k_first == q_last).astype(jnp.int32)
        for k in range(rounds, entries):
            out_ref[2 + 2 * rounds + k] = table_ref[base + k]

    return pl.pallas_call(
        kernel,
        out_shape=jax.ShapeDtypeStruct((2 + 2 * rounds + entries,), jnp.int32),
        in_specs=[in_smem] * 4,
        out_specs=in_smem,
        compiler_params=pltpu.CompilerParams(vmem_limit_bytes=SMALL_VMEM),
    )(place, table, documents, readers)


def choose(info, entry, candidates, after=()):
    numbers = sorted(candidates)

    def kernel(info_ref, *refs):
        named = info_ref[entry]

        @pl.when(named <= numbers[0])
        def _():
            refs[-1][...] = refs[0][...]

        for number, ref in zip(numbers[1:], refs[1 : len(numbers)]):

            @pl.when(named == number)
            def _(ref=ref):
                refs[-1][...] = ref[...]

    first = candidates[numbers[0]]
    return pl.pallas_call(
        kernel,
        out_shape=jax.ShapeDtypeStruct(first.shape, first.dtype),
        in_specs=[in_smem] + [in_vmem] * len(numbers) + [anywhere] * len(after),
        out_specs=in_vmem,
        compiler_params=pltpu.CompilerParams(vmem_limit_bytes=SMALL_VMEM),
        cost_estimate=pl.CostEstimate(
            flops=0, bytes_accessed=4 * first.size, transcendentals=0
        ),
    )(info, *[candidates[n] for n in numbers], *after)


def attend(info, doc_rows, queries, heads, blocks, chosen, state, final):
    slots = len(queries)
    arrays = list({id(array): array for array, _ in queries}.values())
    spots = [([id(a) for a in arrays].index(id(array)), row) for array, row in queries]
    sizes = [part.shape[0] for part in blocks[0]]
    rows = sum(sizes)
    tokens = rows // slots
    all_heads = arrays[0].shape[1] // (GROUP * HEAD_WIDTH)
    count = len(blocks)
    stacked = all_heads * GROUP * rows
    parts = len(sizes)
    with_own = state is None

    def kernel(info_ref, rows_ref, *refs):
        q_refs, refs = refs[: len(arrays)], refs[len(arrays) :]
        kv_refs, refs = refs[: count * parts], refs[count * parts :]
        if final:
            acc, top, *out_refs = refs[:-4]
        else:
            acc, top = refs[-6:-4]
        held, bias, key_bias, query_mask = refs[-4:]
        ctx, head = info_ref[0], info_ref[1]
        chip = head - head % 2

        def docs_of(block, place):
            return rows_ref[pl.ds(block * slots + place, 1), :]

        def make_bias():
            def of_queries(i, _):
                place_q = head ^ i
                q_docs = jnp.broadcast_to(docs_of(ctx, place_q), (tokens, tokens)).T
                q_pos = place_q * tokens + lax.broadcasted_iota(jnp.int32, (tokens, tokens), 0)
                for j in range(slots):
                    place_k = chip ^ j
                    k_pos = place_k * tokens + lax.broadcasted_iota(jnp.int32, (tokens, tokens), 1)
                    seen = (q_docs == docs_of(ctx, place_k)) & (k_pos <= q_pos)
                    bias[
                        pl.ds(pl.multiple_of(i * tokens, tokens), tokens),
                        j * tokens : (j + 1) * tokens,
                    ] = jnp.where(seen, 0.0, neg_large)
                return 0

            lax.fori_loop(0, slots, of_queries, 0)

        def make_masks(block):
            first_doc = docs_of(ctx, 0)[:, 0:1]
            for j in range(slots):
                seen = docs_of(block, chip ^ j) == first_doc
                key_bias[:, j * tokens : (j + 1) * tokens] = jnp.where(seen, 0.0, neg_large)
                asks = (docs_of(ctx, head ^ j) == first_doc).astype(jnp.float32)
                query_mask[j * tokens : (j + 1) * tokens, :] = jnp.broadcast_to(
                    asks, (tokens, tokens)
                ).T

        def lanes_of(head):
            return pl.ds(pl.multiple_of(head * HEAD_WIDTH, HEAD_WIDTH), HEAD_WIDTH)

        def rows_of(n, r):
            return pl.ds(pl.multiple_of(n * rows + r * tokens, tokens), tokens)

        def load(index, kv_head):
            row = 0
            for ref, size in zip(kv_refs[index * parts : (index + 1) * parts], sizes):
                for column, source in enumerate((kv_head, all_heads + kv_head)):
                    held[row : row + size, column * HEAD_WIDTH : (column + 1) * HEAD_WIDTH] = ref[
                        :, lanes_of(source)
                    ]
                row += size

        def give(n, r, sums):
            out_refs[r][:, lanes_of(n - heads[0] * GROUP)] = (
                sums[:, :HEAD_WIDTH] / sums[:, HEAD_WIDTH:]
            ).astype(jnp.bfloat16)

        def tile(n, r, key, keys, masked, first):
            part = rows_of(n, r)
            array, row = spots[r]
            scores = lax.dot_general(
                q_refs[array][row : row + tokens, lanes_of(n)],
                held[key : key + keys, :HEAD_WIDTH],
                (((1,), (1,)), ((), ())),
                preferred_element_type=jnp.float32,
            )
            here = slice(r * tokens, (r + 1) * tokens)
            if first:
                scores = scores + bias[here, key : key + keys]
            elif masked:
                scores = scores + key_bias[...]
            peak = jnp.max(scores, axis=1, keepdims=True)
            peak = jnp.broadcast_to(peak, (tokens, HEAD_WIDTH))
            if not first:
                before = top[part, :]
                peak = jnp.maximum(peak, before)
            weights = jnp.exp2(
                (scores - jnp.concatenate([peak] * (keys // HEAD_WIDTH), axis=1)) * log_scale
            )
            sums = jnp.dot(
                weights.astype(jnp.bfloat16),
                held[key : key + keys, HEAD_WIDTH:],
                preferred_element_type=jnp.float32,
            )
            if not first:
                fade = jnp.exp2((before - peak) * log_scale)
                old = acc[part, :]
                sums = old * jnp.concatenate([fade, fade], axis=1) + sums
                if masked:
                    asks = query_mask[here, :] > 0.5
                    sums = jnp.where(jnp.concatenate([asks, asks], axis=1), sums, old)
                    peak = jnp.where(asks, peak, before)
            if final:
                give(n, r, sums)
            else:
                acc[part, :] = sums
                top[part, :] = peak

        def each_head(work):
            def body(kv_head, _):
                work(kv_head)
                return 0

            lax.fori_loop(heads[0], heads[-1] + 1, body, 0)

        def run(index, masked, first=False):
            def work(kv_head):
                load(index, kv_head)
                for g in range(GROUP):
                    for r in range(slots):
                        tile(kv_head * GROUP + g, r, 0, rows, masked, first)

            each_head(work)

        def run_own():
            make_bias()
            if slots != 4:
                run(0, True, True)
                return
            half = 2 * tokens

            def all_of(chip_first):
                def work(kv_head):
                    load(0, kv_head)
                    for g in range(GROUP):
                        for r in range(slots):
                            n = kv_head * GROUP + g
                            if chip_first == (r < 2):
                                tile(n, r, half * (r >= 2), half, True, True)
                            else:
                                tile(n, r, 0, rows, True, True)

                each_head(work)

            pl.when(chip == 0)(functools.partial(all_of, True))
            pl.when(chip != 0)(functools.partial(all_of, False))

        held[:, 2 * HEAD_WIDTH :] = jnp.ones((rows, HEAD_WIDTH), jnp.bfloat16)
        for index, slot in enumerate(chosen):
            if slot == 0:
                run_own()
                continue
            block, live, full = [info_ref[3 * slot - 1 + i] for i in range(3)]

            @pl.when((live != 0) & (full != 0))
            def _(index=index):
                run(index, False)

            @pl.when((live != 0) & (full == 0))
            def _(index=index, block=block):
                make_masks(block)
                run(index, True)

            if final:

                @pl.when(live == 0)
                def _():
                    def work(kv_head):
                        for n in (kv_head * GROUP + g for g in range(GROUP)):
                            for r in range(slots):
                                give(n, r, acc[rows_of(n, r), :])

                    each_head(work)

    operands = [info, doc_rows] + arrays + [part for block in blocks for part in block]
    aliases = {}
    if not with_own:
        if not final:
            aliases = {len(operands): 0, len(operands) + 1: 1}
        operands += list(state)
    if final:
        out_shape = [
            jax.ShapeDtypeStruct((tokens, len(heads) * GROUP * HEAD_WIDTH), jnp.bfloat16)
        ] * slots
    else:
        out_shape = [
            jax.ShapeDtypeStruct((stacked, 2 * HEAD_WIDTH), jnp.float32),
            jax.ShapeDtypeStruct((stacked, HEAD_WIDTH), jnp.float32),
        ]
    scores_made = len(heads) * GROUP * rows * rows * count
    scratch = 2 * 3 * rows * HEAD_WIDTH + 4 * rows * (2 * HEAD_WIDTH + rows * with_own)
    return pl.pallas_call(
        kernel,
        out_shape=out_shape,
        in_specs=[in_smem] + [in_vmem] * (len(operands) - 1),
        out_specs=[in_vmem] * len(out_shape),
        input_output_aliases=aliases,
        scratch_shapes=[
            pltpu.VMEM((rows, 3 * HEAD_WIDTH), jnp.bfloat16),
            pltpu.VMEM((rows, rows if with_own else HEAD_WIDTH), jnp.float32),
            pltpu.VMEM((1, rows), jnp.float32),
            pltpu.VMEM((rows, tokens), jnp.float32),
        ],
        compiler_params=pltpu.CompilerParams(vmem_limit_bytes=SMALL_VMEM + scratch),
        cost_estimate=pl.CostEstimate(
            flops=4 * scores_made * HEAD_WIDTH,
            bytes_accessed=4 * stacked * HEAD_WIDTH,
            transcendentals=scores_made,
        ),
    )(*operands)


def per_device(query_matrix, key_matrix, value_matrix, documents, readers):
    shards = lax.axis_size("ctx")
    slots = lax.axis_size("head")
    window = readers.shape[1]
    tokens = query_matrix.shape[0]
    local_keys = key_matrix.shape[1] // slots
    local_queries = GROUP * local_keys
    key_heads = local_keys // HEAD_WIDTH
    place = jnp.stack([lax.axis_index("ctx"), lax.axis_index("head")]).astype(jnp.int32)
    doc_rows = documents.reshape(shards * slots, tokens)
    groups = [g for g in (range(2), range(2, slots)) if len(g)]

    plans = [
        [plan_rounds(shards, window, kind, part == len(groups) - 1) for kind in (0, 1)]
        for part in range(len(groups))
    ]
    length = max(len(kind) for plan in plans for kind in plan)
    plans = [[kind + [{}] * (length - len(kind)) for kind in plan] for plan in plans]
    entries = length * (1 + len(plans))
    table = []
    for c in range(shards):
        for h in range(slots):
            brought = [
                [plan[h % 2][k][c][1] if c in plan[h % 2][k] else -1 for k in range(length)]
                for plan in plans
            ]
            assert all(blocks == brought[0] for blocks in brought)
            table += brought[0]
            for plan in plans:
                for k in range(length):
                    sends = [e[2] for e in plan[h % 2][k].values() if e[0] == c]
                    table.append(sends[0] if sends else -1)
    info = survey(
        place, jnp.array(table, jnp.int32), documents, readers.reshape(-1), entries, length, window,
        slots, slots * tokens,
    )

    def swap(value, r):
        return lax.ppermute(value, "head", [(h, h ^ r) for h in range(slots)])

    def exchanged(sources, widths, before=()):
        copies = []
        for r in range(slots):
            column = 0
            for source, width in enumerate(widths):
                target, row = (r, 0) if r < 2 else (1 + r // 2, r % 2 * tokens)
                copies.append(
                    (
                        source,
                        0,
                        tokens,
                        lambda h, r=r, width=width: (h ^ r) * width,
                        width,
                        target,
                        row,
                        column,
                    )
                )
                column += width
        shapes = [(tokens, sum(widths))] * 2 + [(2 * tokens, sum(widths))] * (slots // 2 - 1)
        pieces = move(place, sources, copies, shapes[: slots // 2 + 1], in_vmem, in_vmem)
        spots = {0: (pieces[0], 0), 1: (swap(pieces[1], 1), 0)}
        sent = pieces[2:]
        if before and sent:
            sent = lax.optimization_barrier((tuple(sent), *before))[0]
        for r in range(2, slots, 2):
            spots[r] = (swap(sent[r // 2 - 1], r), 0)
        return spots

    def shared(spots, after=()):
        for r in range(2, slots, 2):
            got = spots[r][0]
            if after:
                got = lax.optimization_barrier((got, *after))[0]
            spots[r] = (got, 0)
            spots[r + 1] = (swap(got[tokens:], 1), 0)

    def part_of(spots, group, after=()):
        return move(
            place,
            [spots[r][0] for r in group],
            [
                (
                    number,
                    spots[r][1],
                    tokens,
                    0,
                    2 * local_keys,
                    0,
                    lambda h, r=r: ((h % 2) ^ r) * tokens - group[0] * tokens,
                    0,
                )
                for number, r in enumerate(group)
            ],
            [(len(group) * tokens, 2 * local_keys)],
            in_vmem,
            in_vmem,
            after,
        )[0]

    def send(part, k, after=()):
        pairs, used = [], set()
        for h in range(slots):
            for target, (source, _, slot) in plans[part][h % 2][k].items():
                pairs.append((h * shards + source, h * shards + target))
                used.add(slot)
        if len(used) > 1:
            candidates = {slot: held[part][slot] for slot in used}
            operand = choose(info, 2 + 3 * length + part * length + k, candidates, after)
        else:
            operand = held[part][min(used)]
            if after:
                operand = lax.optimization_barrier((operand, *after))[0]
        held[part][k + 1] = lax.ppermute(operand, ("head", "ctx"), pairs)
        return operand

    def attended(heads, chosen, state, final=False):
        asked = [queries[r] for r in range(slots)]
        blocks = [[part[slot] for part in held] for slot in chosen]
        return attend(info, doc_rows, asked, heads, blocks, chosen, state, final)

    halves = [range(key_heads)]
    if key_heads % 2 == 0:
        halves = [range(key_heads // 2), range(key_heads // 2, key_heads)]
    later = range(1, len(groups))
    spots = exchanged([key_matrix, value_matrix], [local_keys] * 2)
    held = [{0: part_of(spots, groups[0])}]
    send(0, 0)
    send(0, 1)
    across = range(2, slots, 2)
    queries = exchanged([query_matrix], [local_queries], [spots[r][0] for r in across])
    arrived = [queries[r][0] for r in across]
    shared(spots, [queries[0][0], info])
    for part in later:
        held.append({0: part_of(spots, groups[part], [held[0][1]])})
        send(part, 0)
    shared(queries)
    send(0, 2, arrived)
    for part in later:
        send(part, 1, [held[0][2]])
        for k in range(3, length):
            send(part, k)
    state = attended(range(key_heads), [0, 1], None)
    for k in range(3, length):
        send(0, k, [state[1]])
    for part in later:
        extra = [held[part][k + 1] for k in range(3, length)]
        send(part, 2, [held[0][3]] + extra + [state[1]])
    state = attended(range(key_heads), [2] + list(range(4, length + 1)), state)
    results = []
    for heads in halves:
        outs = attended(heads, [3], state, True)
        results += [swap(outs[r], r) if r else outs[r] for r in range(slots)]
    half_queries = local_queries // len(halves)
    return move(
        place,
        results,
        [
            (
                number * slots + r,
                0,
                tokens,
                0,
                half_queries,
                0,
                0,
                lambda h, r=r, number=number: (h ^ r) * local_queries + number * half_queries,
            )
            for number in range(len(halves))
            for r in range(slots)
        ],
        [query_matrix.shape],
        in_vmem,
        anywhere,
    )[0]


def solution(mesh):
    placed = (
        P(("ctx", "head"), None),
        P(("ctx", "head"), None),
        P(("ctx", "head"), None),
        P(),
        P(),
    )
    return jax.shard_map(
        per_device, mesh=mesh, in_specs=placed, out_specs=P(("ctx", "head"), None), check_vma=False
    )
```

```python
import functools
import math

import jax
import jax.numpy as jnp
from jax import lax
from jax.experimental import pallas as pl
from jax.experimental.pallas import tpu as pltpu
from jax.sharding import PartitionSpec as P

QUERY_HEADS = 32
KEY_VALUE_HEADS = 16
HEAD_WIDTH = 128
GROUP = QUERY_HEADS // KEY_VALUE_HEADS

log_scale = 168.0 ** (-0.5) * math.log2(math.e)
neg_large = -1e30
SMALL_VMEM = 4 * 1024 * 1024


def wanted_blocks(count, window):
    middle = count // 2
    whole = set(range(window)) | set(range(max(middle - window, 0), middle + 1))
    return [
        [b for b in range(max(0, t - window + 1), t) if all(m in whole for m in range(b + 1, t))]
        for t in range(count)
    ]


def plan_rounds(count, window, kind, direct):
    wanted = wanted_blocks(count, window)
    held = [{c: 0} for c in range(count)]
    rounds = []

    def missing(t):
        return [b for b in wanted[t] if b not in held[t]]

    def send(k, s, t, b):
        rounds[k][t] = (s, b, held[s][b])
        held[t][b] = k + 1

    def free(k, s, t):
        return t not in rounds[k] and all(entry[0] != s for entry in rounds[k].values())

    for k in range(4):
        rounds.append({})
        had = [dict(x) for x in held]
        for s in range(count):
            t = s + 2 if k in ((0, 3) if kind == 0 else (1,)) else s ^ 1
            if t >= count or (k == 2 and (kind == 1 or s % 2 == 0)):
                continue
            choice = [b for b in had[s] if b in missing(t) and (k > 1 or b == s)]
            if choice:
                send(k, s, t, max(choice))
    for t in range(count):
        for b in missing(t):
            options = [(k, b) for k in (kind,) if t - b == 1 and free(k, b, t)]
            k = 4
            while not options:
                if k == len(rounds):
                    rounds.append({})
                holders = [s for s in range(count) if held[s].get(b, k + 1) <= k and free(k, s, t)]
                if direct:
                    holders = [s for s in holders if s == b]
                holders.sort(key=lambda s: (abs(t - s) != 2, abs(t - s)))
                options = [(k, s) for s in holders]
                k += 1
            send(options[0][0], options[0][1], t, b)
    return rounds


in_smem = pl.BlockSpec(memory_space=pltpu.SMEM)
in_vmem = pl.BlockSpec(memory_space=pltpu.VMEM)
anywhere = pl.BlockSpec(memory_space=pl.ANY)
in_hbm = pl.BlockSpec(memory_space=pltpu.HBM)


def move(place, operands, copies, shapes, source_spec, target_spec, after=(), into=()):
    count_in = len(operands)

    def kernel(place_ref, *refs):
        h = place_ref[1]
        sources, targets, sems = refs[:count_in], refs[-1 - len(shapes) : -1], refs[-1]

        def span(value, size):
            return pl.ds(pl.multiple_of(value(h), 128) if callable(value) else value, size)

        started = []
        for number, (s, row, rows, col, cols, t, to_row, to_col) in enumerate(copies):
            copy = pltpu.make_async_copy(
                sources[s].at[span(row, rows), span(col, cols)],
                targets[t].at[span(to_row, rows), span(to_col, cols)],
                sems.at[number],
            )
            copy.start()
            started.append(copy)
        for copy in started:
            copy.wait()

    return pl.pallas_call(
        kernel,
        out_shape=[jax.ShapeDtypeStruct(s, jnp.bfloat16) for s in shapes],
        in_specs=[in_smem]
        + [source_spec] * count_in
        + [anywhere] * len(after)
        + [target_spec] * len(into),
        out_specs=[target_spec] * len(shapes),
        input_output_aliases={1 + count_in + len(after) + i: i for i in range(len(into))},
        scratch_shapes=[pltpu.SemaphoreType.DMA((len(copies),))],
        compiler_params=pltpu.CompilerParams(
            vmem_limit_bytes=SMALL_VMEM
        ),
        cost_estimate=pl.CostEstimate(
            flops=0,
            bytes_accessed=sum(4 * c[2] * c[4] for c in copies),
            transcendentals=0,
        ),
    )(place, *operands, *after, *into)


def survey(place, table, documents, readers, entries, rounds, window, slots, rows):
    def kernel(place_ref, table_ref, doc_ref, read_ref, out_ref):
        ctx, head = place_ref[0], place_ref[1]
        out_ref[0] = ctx
        out_ref[1] = head
        base = (ctx * slots + head) * entries
        q_first, q_last = doc_ref[ctx * rows], doc_ref[ctx * rows + rows - 1]
        for k in range(rounds):
            number = table_ref[base + k]
            block = jnp.maximum(number, 0)
            k_first, k_last = doc_ref[block * rows], doc_ref[block * rows + rows - 1]
            distance = jnp.clip(ctx - block, 0, window - 1)
            live = (
                (number >= 0) & (read_ref[distance, block] > 0) & (k_last == q_first)
            )
            out_ref[2 + 3 * k] = block
            out_ref[3 + 3 * k] = live.astype(jnp.int32)
            out_ref[4 + 3 * k] = (k_first == q_last).astype(jnp.int32)
        for k in range(rounds, entries):
            out_ref[2 + 2 * rounds + k] = table_ref[base + k]

    return pl.pallas_call(
        kernel,
        out_shape=jax.ShapeDtypeStruct((2 + 2 * rounds + entries,), jnp.int32),
        in_specs=[in_smem] * 4,
        out_specs=in_smem,
        compiler_params=pltpu.CompilerParams(vmem_limit_bytes=SMALL_VMEM),
    )(place, table, documents, readers)


def choose(info, entry, candidates, after=()):
    numbers = sorted(candidates)

    def kernel(info_ref, *refs):
        named = info_ref[entry]

        @pl.when(named <= numbers[0])
        def _():
            refs[-1][...] = refs[0][...]

        for number, ref in zip(numbers[1:], refs[1 : len(numbers)]):

            @pl.when(named == number)
            def _(ref=ref):
                refs[-1][...] = ref[...]

    first = candidates[numbers[0]]
    return pl.pallas_call(
        kernel,
        out_shape=jax.ShapeDtypeStruct(first.shape, first.dtype),
        in_specs=[in_smem] + [in_vmem] * len(numbers) + [anywhere] * len(after),
        out_specs=in_vmem,
        compiler_params=pltpu.CompilerParams(vmem_limit_bytes=SMALL_VMEM),
        cost_estimate=pl.CostEstimate(
            flops=0, bytes_accessed=4 * first.size, transcendentals=0
        ),
    )(info, *[candidates[n] for n in numbers], *after)


def attend(info, doc_rows, queries, heads, blocks, chosen, state, final):
    slots = len(queries)
    arrays = list({id(array): array for array, _ in queries}.values())
    spots = [([id(a) for a in arrays].index(id(array)), row) for array, row in queries]
    sizes = [part.shape[0] for part in blocks[0]]
    rows = sum(sizes)
    tokens = rows // slots
    all_heads = arrays[0].shape[1] // (GROUP * HEAD_WIDTH)
    count = len(blocks)
    stacked = all_heads * GROUP * rows
    parts = len(sizes)
    with_own = state is None

    def kernel(info_ref, rows_ref, *refs):
        q_refs, refs = refs[: len(arrays)], refs[len(arrays) :]
        kv_refs, refs = refs[: count * parts], refs[count * parts :]
        if final:
            acc, top, *out_refs = refs[:-4]
        else:
            acc, top = refs[-6:-4]
        held, bias, key_bias, query_mask = refs[-4:]
        ctx, head = info_ref[0], info_ref[1]
        chip = head - head % 2

        def docs_of(block, place):
            return rows_ref[pl.ds(block * slots + place, 1), :]

        def make_bias():
            def of_queries(i, _):
                place_q = head ^ i
                q_docs = jnp.broadcast_to(docs_of(ctx, place_q), (tokens, tokens)).T
                q_pos = place_q * tokens + lax.broadcasted_iota(jnp.int32, (tokens, tokens), 0)
                for j in range(slots):
                    place_k = chip ^ j
                    k_pos = place_k * tokens + lax.broadcasted_iota(jnp.int32, (tokens, tokens), 1)
                    seen = (q_docs == docs_of(ctx, place_k)) & (k_pos <= q_pos)
                    bias[
                        pl.ds(pl.multiple_of(i * tokens, tokens), tokens),
                        j * tokens : (j + 1) * tokens,
                    ] = jnp.where(seen, 0.0, neg_large)
                return 0

            lax.fori_loop(0, slots, of_queries, 0)

        def make_masks(block):
            first_doc = docs_of(ctx, 0)[:, 0:1]
            for j in range(slots):
                seen = docs_of(block, chip ^ j) == first_doc
                key_bias[:, j * tokens : (j + 1) * tokens] = jnp.where(seen, 0.0, neg_large)
                asks = (docs_of(ctx, head ^ j) == first_doc).astype(jnp.float32)
                query_mask[j * tokens : (j + 1) * tokens, :] = jnp.broadcast_to(
                    asks, (tokens, tokens)
                ).T

        def lanes_of(head):
            return pl.ds(pl.multiple_of(head * HEAD_WIDTH, HEAD_WIDTH), HEAD_WIDTH)

        def rows_of(n, r):
            return pl.ds(pl.multiple_of(n * rows + r * tokens, tokens), tokens)

        def load(index, kv_head):
            row = 0
            for ref, size in zip(kv_refs[index * parts : (index + 1) * parts], sizes):
                for column, source in enumerate((kv_head, all_heads + kv_head)):
                    held[row : row + size, column * HEAD_WIDTH : (column + 1) * HEAD_WIDTH] = ref[
                        :, lanes_of(source)
                    ]
                row += size

        def give(n, r, sums):
            out_refs[final.index(r)][:, lanes_of(n - heads[0] * GROUP)] = (
                sums[:, :HEAD_WIDTH] / sums[:, HEAD_WIDTH:]
            ).astype(jnp.bfloat16)

        def tile(n, r, key, keys, masked, first):
            part = rows_of(n, r)
            array, row = spots[r]
            scores = lax.dot_general(
                q_refs[array][row : row + tokens, lanes_of(n)],
                held[key : key + keys, :HEAD_WIDTH],
                (((1,), (1,)), ((), ())),
                preferred_element_type=jnp.float32,
            )
            here = slice(r * tokens, (r + 1) * tokens)
            if first:
                scores = scores + bias[here, key : key + keys]
            elif masked:
                scores = scores + key_bias[...]
            peak = jnp.max(scores, axis=1, keepdims=True)
            peak = jnp.broadcast_to(peak, (tokens, HEAD_WIDTH))
            if not first:
                before = top[part, :]
                peak = jnp.maximum(peak, before)
            weights = jnp.exp2(
                (scores - jnp.concatenate([peak] * (keys // HEAD_WIDTH), axis=1)) * log_scale
            )
            sums = jnp.dot(
                weights.astype(jnp.bfloat16),
                held[key : key + keys, HEAD_WIDTH:],
                preferred_element_type=jnp.float32,
            )
            if not first:
                fade = jnp.exp2((before - peak) * log_scale)
                old = acc[part, :]
                sums = old * jnp.concatenate([fade, fade], axis=1) + sums
                if masked:
                    asks = query_mask[here, :] > 0.5
                    sums = jnp.where(jnp.concatenate([asks, asks], axis=1), sums, old)
                    peak = jnp.where(asks, peak, before)
            if final:
                give(n, r, sums)
            else:
                acc[part, :] = sums
                top[part, :] = peak

        def each_head(work):
            def body(kv_head, _):
                work(kv_head)
                return 0

            lax.fori_loop(heads[0], heads[-1] + 1, body, 0)

        def run(index, masked, first=False):
            def work(kv_head):
                load(index, kv_head)
                for g in range(GROUP):
                    for r in final or range(slots):
                        tile(kv_head * GROUP + g, r, 0, rows, masked, first)

            each_head(work)

        def run_own():
            make_bias()
            if slots != 4:
                run(0, True, True)
                return
            half = 2 * tokens

            def all_of(chip_first):
                def work(kv_head):
                    load(0, kv_head)
                    for g in range(GROUP):
                        for r in range(slots):
                            n = kv_head * GROUP + g
                            if chip_first == (r < 2):
                                tile(n, r, half * (r >= 2), half, True, True)
                            else:
                                tile(n, r, 0, rows, True, True)

                each_head(work)

            pl.when(chip == 0)(functools.partial(all_of, True))
            pl.when(chip != 0)(functools.partial(all_of, False))

        held[:, 2 * HEAD_WIDTH :] = jnp.ones((rows, HEAD_WIDTH), jnp.bfloat16)
        for index, slot in enumerate(chosen):
            if slot == 0:
                run_own()
                continue
            slot, *guard = slot if isinstance(slot, tuple) else (slot,)
            block, live, full = [info_ref[3 * slot - 1 + i] for i in range(3)]
            if guard:
                other = info_ref[3 * guard[0]]
                live = jnp.where((other != 0) == guard[1], live, 0)

            @pl.when((live != 0) & (full != 0))
            def _(index=index):
                run(index, False)

            @pl.when((live != 0) & (full == 0))
            def _(index=index, block=block):
                make_masks(block)
                run(index, True)

            if final:

                @pl.when(live == 0)
                def _():
                    def work(kv_head):
                        for n in (kv_head * GROUP + g for g in range(GROUP)):
                            for r in final:
                                give(n, r, acc[rows_of(n, r), :])

                    each_head(work)

    operands = [info, doc_rows] + arrays + [part for block in blocks for part in block]
    aliases = {}
    if not with_own:
        if not final:
            aliases = {len(operands): 0, len(operands) + 1: 1}
        operands += list(state)
    if final:
        out_shape = [
            jax.ShapeDtypeStruct((tokens, len(heads) * GROUP * HEAD_WIDTH), jnp.bfloat16)
        ] * len(final)
    else:
        out_shape = [
            jax.ShapeDtypeStruct((stacked, 2 * HEAD_WIDTH), jnp.float32),
            jax.ShapeDtypeStruct((stacked, HEAD_WIDTH), jnp.float32),
        ]
    scores_made = len(heads) * GROUP * rows * rows * count
    scratch = 2 * 3 * rows * HEAD_WIDTH + 4 * rows * (2 * HEAD_WIDTH + rows * with_own)
    return pl.pallas_call(
        kernel,
        out_shape=out_shape,
        in_specs=[in_smem] + [in_vmem] * (len(operands) - 1),
        out_specs=[in_vmem] * len(out_shape),
        input_output_aliases=aliases,
        scratch_shapes=[
            pltpu.VMEM((rows, 3 * HEAD_WIDTH), jnp.bfloat16),
            pltpu.VMEM((rows, rows if with_own else HEAD_WIDTH), jnp.float32),
            pltpu.VMEM((1, rows), jnp.float32),
            pltpu.VMEM((rows, tokens), jnp.float32),
        ],
        compiler_params=pltpu.CompilerParams(vmem_limit_bytes=SMALL_VMEM + scratch),
        cost_estimate=pl.CostEstimate(
            flops=2 * scores_made * HEAD_WIDTH,
            bytes_accessed=4 * stacked * HEAD_WIDTH,
            transcendentals=scores_made,
        ),
    )(*operands)


def per_device(query_matrix, key_matrix, value_matrix, documents, readers):
    shards = lax.axis_size("ctx")
    slots = lax.axis_size("head")
    window = readers.shape[1]
    tokens = query_matrix.shape[0]
    local_keys = key_matrix.shape[1] // slots
    local_queries = GROUP * local_keys
    key_heads = local_keys // HEAD_WIDTH
    place = jnp.stack([lax.axis_index("ctx"), lax.axis_index("head")]).astype(jnp.int32)
    doc_rows = documents.reshape(shards * slots, tokens)
    groups = [g for g in (range(2), range(2, slots)) if len(g)]

    plans = [
        [plan_rounds(shards, window, kind, part == len(groups) - 1) for kind in (0, 1)]
        for part in range(len(groups))
    ]
    length = max(len(kind) for plan in plans for kind in plan)
    plans = [[kind + [{}] * (length - len(kind)) for kind in plan] for plan in plans]
    entries = length * (1 + len(plans))
    table = []
    for c in range(shards):
        for h in range(slots):
            brought = [
                [plan[h % 2][k][c][1] if c in plan[h % 2][k] else -1 for k in range(length)]
                for plan in plans
            ]
            assert all(blocks == brought[0] for blocks in brought)
            table += brought[0]
            for plan in plans:
                for k in range(length):
                    sends = [e[2] for e in plan[h % 2][k].values() if e[0] == c]
                    table.append(sends[0] if sends else -1)
    info = survey(
        place, jnp.array(table, jnp.int32), documents, readers.T, entries, length, window,
        slots, slots * tokens,
    )

    def swap(value, r):
        return lax.ppermute(value, "head", [(h, h ^ r) for h in range(slots)])

    def exchanged(sources, widths, before=()):
        copies = []
        for r in range(slots):
            column = 0
            for source, width in enumerate(widths):
                target, row = (r, 0) if r < 2 else (1 + r // 2, r % 2 * tokens)
                copies.append(
                    (
                        source,
                        0,
                        tokens,
                        lambda h, r=r, width=width: (h ^ r) * width,
                        width,
                        target,
                        row,
                        column,
                    )
                )
                column += width
        shapes = [(tokens, sum(widths))] * 2 + [(2 * tokens, sum(widths))] * (slots // 2 - 1)
        pieces = move(place, sources, copies, shapes[: slots // 2 + 1], in_vmem, in_vmem)
        spots = {0: (pieces[0], 0), 1: (swap(pieces[1], 1), 0)}
        sent = pieces[2:]
        if before and sent:
            sent = lax.optimization_barrier((tuple(sent), *before))[0]
        for r in range(2, slots, 2):
            spots[r] = (swap(sent[r // 2 - 1], r), 0)
        return spots

    def shared(spots, after=()):
        for r in range(2, slots, 2):
            got = spots[r][0]
            if after:
                got = lax.optimization_barrier((got, *after))[0]
            spots[r] = (got, 0)
            spots[r + 1] = (swap(got[tokens:], 1), 0)

    def part_of(spots, group, after=()):
        return move(
            place,
            [spots[r][0] for r in group],
            [
                (
                    number,
                    spots[r][1],
                    tokens,
                    0,
                    2 * local_keys,
                    0,
                    lambda h, r=r: ((h % 2) ^ r) * tokens - group[0] * tokens,
                    0,
                )
                for number, r in enumerate(group)
            ],
            [(len(group) * tokens, 2 * local_keys)],
            in_vmem,
            in_vmem,
            after,
        )[0]

    def send(part, k, after=()):
        pairs, used = [], set()
        for h in range(slots):
            for target, (source, _, slot) in plans[part][h % 2][k].items():
                pairs.append((h * shards + source, h * shards + target))
                used.add(slot)
        if len(used) > 1:
            candidates = {slot: held[part][slot] for slot in used}
            operand = choose(info, 2 + 3 * length + part * length + k, candidates, after)
        else:
            operand = held[part][min(used)]
            if after:
                operand = lax.optimization_barrier((operand, *after))[0]
        held[part][k + 1] = lax.ppermute(operand, ("head", "ctx"), pairs)
        return operand

    def attended(heads, chosen, state, final=None):
        asked = [queries[r] for r in range(slots)]
        plain = [slot[0] if isinstance(slot, tuple) else slot for slot in chosen]
        blocks = [[part[slot] for part in held] for slot in plain]
        return attend(info, doc_rows, asked, heads, blocks, chosen, state, final)

    halves = [range(key_heads)]
    if key_heads % 2 == 0:
        halves = [range(key_heads // 2), range(key_heads // 2, key_heads)]
    later = range(1, len(groups))
    spots = exchanged([key_matrix, value_matrix], [local_keys] * 2)
    held = [{0: part_of(spots, groups[0])}]
    send(0, 0)
    send(0, 1, [info])
    across = range(2, slots, 2)
    queries = exchanged([query_matrix], [local_queries], [spots[r][0] for r in across])
    arrived = [queries[r][0] for r in across]
    shared(spots, [queries[0][0]])
    for part in later:
        held.append({0: part_of(spots, groups[part], [held[0][1], held[0][2]])})
        send(part, 0)
        send(part, 1)
    shared(queries)
    send(0, 2)
    state = attended(range(key_heads), [0], None)
    send(0, 3, arrived)
    more = range(4, length)
    for part in later:
        for k in more:
            send(part, k)
        send(part, 2, [held[part][2], state[1]] + [held[part][k + 1] for k in more])
    state = attended(range(key_heads), [1, (2, 1, False)], state)
    for k in more:
        send(0, k, [state[1]])
    for part in later:
        send(part, 3, [held[0][4], state[1]])
    state = attended(
        range(key_heads), [(2, 1, True), 3] + [k + 1 for k in more], state
    )
    results = []
    others = list(range(1, slots))
    for heads in halves:
        outs = attended(heads, [4], state, others)
        results.append([(swap(out, r), r, heads[0]) for r, out in zip(others, outs)])
    results[0].append((attended(range(key_heads), [4], state, [0])[0], 0, 0))
    whole = ()
    for group in results:
        whole = move(
            place,
            [out for out, _, _ in group],
            [
                (
                    number,
                    0,
                    tokens,
                    0,
                    out.shape[1],
                    0,
                    0,
                    lambda h, r=r, first=first: (h ^ r) * local_queries
                    + first * GROUP * HEAD_WIDTH,
                )
                for number, (out, r, first) in enumerate(group)
            ],
            [query_matrix.shape],
            in_vmem,
            anywhere,
            (),
            whole,
        )
    return whole[0]


def solution(mesh):
    placed = (
        P(("ctx", "head"), None),
        P(("ctx", "head"), None),
        P(("ctx", "head"), None),
        P(),
        P(),
    )
    return jax.shard_map(
        per_device, mesh=mesh, in_specs=placed, out_specs=P(("ctx", "head"), None), check_vma=False
    )
```

```python
import functools
import math

import jax
import jax.numpy as jnp
from jax import lax
from jax.experimental import pallas as pl
from jax.experimental.pallas import tpu as pltpu
from jax.sharding import PartitionSpec as P

QUERY_HEADS = 32
KEY_VALUE_HEADS = 16
HEAD_WIDTH = 128
GROUP = QUERY_HEADS // KEY_VALUE_HEADS

log_scale = 168.0 ** (-0.5) * math.log2(math.e)
neg_large = -1e30
SMALL_VMEM = 4 * 1024 * 1024


def wanted_blocks(count, window):
    middle = count // 2
    whole = set(range(window)) | set(range(max(middle - window, 0), middle + 1))
    return [
        [b for b in range(max(0, t - window + 1), t) if all(m in whole for m in range(b + 1, t))]
        for t in range(count)
    ]


def plan_rounds(count, window, kind, direct):
    wanted = wanted_blocks(count, window)
    held = [{c: 0} for c in range(count)]
    rounds = []

    def missing(t):
        return [b for b in wanted[t] if b not in held[t]]

    def send(k, s, t, b):
        rounds[k][t] = (s, b, held[s][b])
        held[t][b] = k + 1

    def free(k, s, t):
        return t not in rounds[k] and all(entry[0] != s for entry in rounds[k].values())

    for k in range(4):
        rounds.append({})
        had = [dict(x) for x in held]
        for s in range(count):
            t = s + 2 if k in ((0, 3) if kind == 0 else (1,)) else s ^ 1
            if t >= count or (k == 2 and (kind == 1 or s % 2 == 0)):
                continue
            choice = [b for b in had[s] if b in missing(t) and (k > 1 or b == s)]
            if choice:
                send(k, s, t, max(choice))
    for t in range(count):
        for b in missing(t):
            options = [(k, b) for k in (kind,) if t - b == 1 and free(k, b, t)]
            k = 4
            while not options:
                if k == len(rounds):
                    rounds.append({})
                holders = [s for s in range(count) if held[s].get(b, k + 1) <= k and free(k, s, t)]
                if direct:
                    holders = [s for s in holders if s == b]
                holders.sort(key=lambda s: (abs(t - s) != 2, abs(t - s)))
                options = [(k, s) for s in holders]
                k += 1
            send(options[0][0], options[0][1], t, b)
    return rounds


in_smem = pl.BlockSpec(memory_space=pltpu.SMEM)
in_vmem = pl.BlockSpec(memory_space=pltpu.VMEM)
anywhere = pl.BlockSpec(memory_space=pl.ANY)
in_hbm = pl.BlockSpec(memory_space=pltpu.HBM)


def move(place, operands, copies, shapes, source_spec, target_spec, after=(), into=()):
    count_in = len(operands)

    def kernel(place_ref, *refs):
        h = place_ref[1]
        sources, targets, sems = refs[:count_in], refs[-1 - len(shapes) : -1], refs[-1]

        def span(value, size):
            return pl.ds(pl.multiple_of(value(h), 128) if callable(value) else value, size)

        started = []
        for number, (s, row, rows, col, cols, t, to_row, to_col) in enumerate(copies):
            copy = pltpu.make_async_copy(
                sources[s].at[span(row, rows), span(col, cols)],
                targets[t].at[span(to_row, rows), span(to_col, cols)],
                sems.at[number],
            )
            copy.start()
            started.append(copy)
        for copy in started:
            copy.wait()

    return pl.pallas_call(
        kernel,
        out_shape=[jax.ShapeDtypeStruct(s, jnp.bfloat16) for s in shapes],
        in_specs=[in_smem]
        + [source_spec] * count_in
        + [anywhere] * len(after)
        + [target_spec] * len(into),
        out_specs=[target_spec] * len(shapes),
        input_output_aliases={1 + count_in + len(after) + i: i for i in range(len(into))},
        scratch_shapes=[pltpu.SemaphoreType.DMA((len(copies),))],
        compiler_params=pltpu.CompilerParams(
            vmem_limit_bytes=SMALL_VMEM
        ),
        cost_estimate=pl.CostEstimate(
            flops=0,
            bytes_accessed=sum(4 * c[2] * c[4] for c in copies),
            transcendentals=0,
        ),
    )(place, *operands, *after, *into)


def survey(place, table, documents, readers, entries, rounds, window, slots, rows):
    def kernel(place_ref, table_ref, doc_ref, read_ref, out_ref):
        ctx, head = place_ref[0], place_ref[1]
        out_ref[0] = ctx
        out_ref[1] = head
        base = (ctx * slots + head) * entries
        q_first, q_last = doc_ref[ctx * rows], doc_ref[ctx * rows + rows - 1]
        for k in range(rounds):
            number = table_ref[base + k]
            block = jnp.maximum(number, 0)
            k_first, k_last = doc_ref[block * rows], doc_ref[block * rows + rows - 1]
            distance = jnp.clip(ctx - block, 0, window - 1)
            live = (
                (number >= 0) & (read_ref[distance, block] > 0) & (k_last == q_first)
            )
            out_ref[2 + 3 * k] = block
            out_ref[3 + 3 * k] = live.astype(jnp.int32)
            out_ref[4 + 3 * k] = (k_first == q_last).astype(jnp.int32)
        for k in range(rounds, entries):
            out_ref[2 + 2 * rounds + k] = table_ref[base + k]

    return pl.pallas_call(
        kernel,
        out_shape=jax.ShapeDtypeStruct((2 + 2 * rounds + entries,), jnp.int32),
        in_specs=[in_smem] * 4,
        out_specs=in_smem,
        compiler_params=pltpu.CompilerParams(vmem_limit_bytes=SMALL_VMEM),
    )(place, table, documents, readers)


def choose(info, entry, candidates, after=()):
    numbers = sorted(candidates)

    def kernel(info_ref, *refs):
        named = info_ref[entry]

        @pl.when(named <= numbers[0])
        def _():
            refs[-1][...] = refs[0][...]

        for number, ref in zip(numbers[1:], refs[1 : len(numbers)]):

            @pl.when(named == number)
            def _(ref=ref):
                refs[-1][...] = ref[...]

    first = candidates[numbers[0]]
    return pl.pallas_call(
        kernel,
        out_shape=jax.ShapeDtypeStruct(first.shape, first.dtype),
        in_specs=[in_smem] + [in_vmem] * len(numbers) + [anywhere] * len(after),
        out_specs=in_vmem,
        compiler_params=pltpu.CompilerParams(vmem_limit_bytes=SMALL_VMEM),
        cost_estimate=pl.CostEstimate(
            flops=0, bytes_accessed=4 * first.size, transcendentals=0
        ),
    )(info, *[candidates[n] for n in numbers], *after)


def attend(info, doc_rows, queries, heads, blocks, chosen, state, final):
    slots = len(queries)
    arrays = list({id(array): array for array, _ in queries}.values())
    spots = [([id(a) for a in arrays].index(id(array)), row) for array, row in queries]
    sizes = [part.shape[0] for part in blocks[0]]
    rows = sum(sizes)
    tokens = rows // slots
    all_heads = arrays[0].shape[1] // (GROUP * HEAD_WIDTH)
    count = len(blocks)
    stacked = all_heads * GROUP * rows
    parts = len(sizes)
    with_own = state is None

    def kernel(info_ref, rows_ref, *refs):
        q_refs, refs = refs[: len(arrays)], refs[len(arrays) :]
        kv_refs, refs = refs[: count * parts], refs[count * parts :]
        if final:
            acc, top, *out_refs = refs[:-4]
        else:
            acc, top = refs[-6:-4]
        held, bias, key_bias, query_mask = refs[-4:]
        ctx, head = info_ref[0], info_ref[1]
        chip = head - head % 2

        def docs_of(block, place):
            return rows_ref[pl.ds(block * slots + place, 1), :]

        def make_bias():
            def of_queries(i, _):
                place_q = head ^ i
                q_docs = jnp.broadcast_to(docs_of(ctx, place_q), (tokens, tokens)).T
                q_pos = place_q * tokens + lax.broadcasted_iota(jnp.int32, (tokens, tokens), 0)
                for j in range(slots):
                    place_k = chip ^ j
                    k_pos = place_k * tokens + lax.broadcasted_iota(jnp.int32, (tokens, tokens), 1)
                    seen = (q_docs == docs_of(ctx, place_k)) & (k_pos <= q_pos)
                    bias[
                        pl.ds(pl.multiple_of(i * tokens, tokens), tokens),
                        j * tokens : (j + 1) * tokens,
                    ] = jnp.where(seen, 0.0, neg_large)
                return 0

            lax.fori_loop(0, slots, of_queries, 0)

        def make_masks(block):
            first_doc = docs_of(ctx, 0)[:, 0:1]
            for j in range(slots):
                seen = docs_of(block, chip ^ j) == first_doc
                key_bias[:, j * tokens : (j + 1) * tokens] = jnp.where(seen, 0.0, neg_large)
                asks = (docs_of(ctx, head ^ j) == first_doc).astype(jnp.float32)
                query_mask[j * tokens : (j + 1) * tokens, :] = jnp.broadcast_to(
                    asks, (tokens, tokens)
                ).T

        def lanes_of(head):
            return pl.ds(pl.multiple_of(head * HEAD_WIDTH, HEAD_WIDTH), HEAD_WIDTH)

        def rows_of(n, r):
            return pl.ds(pl.multiple_of(n * rows + r * tokens, tokens), tokens)

        def load(index, kv_head):
            row = 0
            for ref, size in zip(kv_refs[index * parts : (index + 1) * parts], sizes):
                for column, source in enumerate((kv_head, all_heads + kv_head)):
                    held[row : row + size, column * HEAD_WIDTH : (column + 1) * HEAD_WIDTH] = ref[
                        :, lanes_of(source)
                    ]
                row += size

        def give(n, r, sums):
            out_refs[final.index(r)][:, lanes_of(n - heads[0] * GROUP)] = (
                sums[:, :HEAD_WIDTH] / sums[:, HEAD_WIDTH:]
            ).astype(jnp.bfloat16)

        def tile(n, r, key, keys, masked, first):
            part = rows_of(n, r)
            array, row = spots[r]
            scores = lax.dot_general(
                q_refs[array][row : row + tokens, lanes_of(n)],
                held[key : key + keys, :HEAD_WIDTH],
                (((1,), (1,)), ((), ())),
                preferred_element_type=jnp.float32,
            )
            here = slice(r * tokens, (r + 1) * tokens)
            if first:
                scores = scores + bias[here, key : key + keys]
            elif masked:
                scores = scores + key_bias[...]
            peak = jnp.max(scores, axis=1, keepdims=True)
            peak = jnp.broadcast_to(peak, (tokens, HEAD_WIDTH))
            if not first:
                before = top[part, :]
                peak = jnp.maximum(peak, before)
            weights = jnp.exp2(
                (scores - jnp.concatenate([peak] * (keys // HEAD_WIDTH), axis=1)) * log_scale
            )
            sums = jnp.dot(
                weights.astype(jnp.bfloat16),
                held[key : key + keys, HEAD_WIDTH:],
                preferred_element_type=jnp.float32,
            )
            if not first:
                fade = jnp.exp2((before - peak) * log_scale)
                old = acc[part, :]
                sums = old * jnp.concatenate([fade, fade], axis=1) + sums
                if masked:
                    asks = query_mask[here, :] > 0.5
                    sums = jnp.where(jnp.concatenate([asks, asks], axis=1), sums, old)
                    peak = jnp.where(asks, peak, before)
            if final:
                give(n, r, sums)
            else:
                acc[part, :] = sums
                top[part, :] = peak

        def each_head(work):
            def body(kv_head, _):
                work(kv_head)
                return 0

            lax.fori_loop(heads[0], heads[-1] + 1, body, 0)

        def run(index, masked, first=False):
            def work(kv_head):
                load(index, kv_head)
                for g in range(GROUP):
                    for r in final or range(slots):
                        tile(kv_head * GROUP + g, r, 0, rows, masked, first)

            each_head(work)

        def run_own():
            make_bias()
            if slots != 4:
                run(0, True, True)
                return
            half = 2 * tokens

            def all_of(chip_first):
                def work(kv_head):
                    load(0, kv_head)
                    for g in range(GROUP):
                        for r in range(slots):
                            n = kv_head * GROUP + g
                            if chip_first == (r < 2):
                                tile(n, r, half * (r >= 2), half, True, True)
                            else:
                                tile(n, r, 0, rows, True, True)

                each_head(work)

            pl.when(chip == 0)(functools.partial(all_of, True))
            pl.when(chip != 0)(functools.partial(all_of, False))

        held[:, 2 * HEAD_WIDTH :] = jnp.ones((rows, HEAD_WIDTH), jnp.bfloat16)
        for index, slot in enumerate(chosen):
            if slot == 0:
                run_own()
                continue
            slot, *guard = slot if isinstance(slot, tuple) else (slot,)
            block, live, full = [info_ref[3 * slot - 1 + i] for i in range(3)]
            if guard:
                other = info_ref[3 * guard[0]]
                live = jnp.where((other != 0) == guard[1], live, 0)

            @pl.when((live != 0) & (full != 0))
            def _(index=index):
                run(index, False)

            @pl.when((live != 0) & (full == 0))
            def _(index=index, block=block):
                make_masks(block)
                run(index, True)

            if final:

                @pl.when(live == 0)
                def _():
                    def work(kv_head):
                        for n in (kv_head * GROUP + g for g in range(GROUP)):
                            for r in final:
                                give(n, r, acc[rows_of(n, r), :])

                    each_head(work)

    operands = [info, doc_rows] + arrays + [part for block in blocks for part in block]
    aliases = {}
    if not with_own:
        if not final:
            aliases = {len(operands): 0, len(operands) + 1: 1}
        operands += list(state)
    if final:
        out_shape = [
            jax.ShapeDtypeStruct((tokens, len(heads) * GROUP * HEAD_WIDTH), jnp.bfloat16)
        ] * len(final)
    else:
        out_shape = [
            jax.ShapeDtypeStruct((stacked, 2 * HEAD_WIDTH), jnp.float32),
            jax.ShapeDtypeStruct((stacked, HEAD_WIDTH), jnp.float32),
        ]
    scores_made = len(heads) * GROUP * rows * rows * count
    scratch = 2 * 3 * rows * HEAD_WIDTH + 4 * rows * (2 * HEAD_WIDTH + rows * with_own)
    return pl.pallas_call(
        kernel,
        out_shape=out_shape,
        in_specs=[in_smem] + [in_vmem] * (len(operands) - 1),
        out_specs=[in_vmem] * len(out_shape),
        input_output_aliases=aliases,
        scratch_shapes=[
            pltpu.VMEM((rows, 3 * HEAD_WIDTH), jnp.bfloat16),
            pltpu.VMEM((rows, rows if with_own else HEAD_WIDTH), jnp.float32),
            pltpu.VMEM((1, rows), jnp.float32),
            pltpu.VMEM((rows, tokens), jnp.float32),
        ],
        compiler_params=pltpu.CompilerParams(vmem_limit_bytes=SMALL_VMEM + scratch),
        cost_estimate=pl.CostEstimate(
            flops=2 * scores_made * HEAD_WIDTH,
            bytes_accessed=4 * stacked * HEAD_WIDTH,
            transcendentals=scores_made,
        ),
    )(*operands)


def per_device(query_matrix, key_matrix, value_matrix, documents, readers):
    shards = lax.axis_size("ctx")
    slots = lax.axis_size("head")
    window = readers.shape[1]
    tokens = query_matrix.shape[0]
    local_keys = key_matrix.shape[1] // slots
    local_queries = GROUP * local_keys
    key_heads = local_keys // HEAD_WIDTH
    place = jnp.stack([lax.axis_index("ctx"), lax.axis_index("head")]).astype(jnp.int32)
    doc_rows = documents.reshape(shards * slots, tokens)
    groups = [g for g in (range(2), range(2, slots)) if len(g)]

    plans = [
        [plan_rounds(shards, window, kind, part == len(groups) - 1) for kind in (0, 1)]
        for part in range(len(groups))
    ]
    length = max(len(kind) for plan in plans for kind in plan)
    plans = [[kind + [{}] * (length - len(kind)) for kind in plan] for plan in plans]
    entries = length * (1 + len(plans))
    table = []
    for c in range(shards):
        for h in range(slots):
            brought = [
                [plan[h % 2][k][c][1] if c in plan[h % 2][k] else -1 for k in range(length)]
                for plan in plans
            ]
            assert all(blocks == brought[0] for blocks in brought)
            table += brought[0]
            for plan in plans:
                for k in range(length):
                    sends = [e[2] for e in plan[h % 2][k].values() if e[0] == c]
                    table.append(sends[0] if sends else -1)
    info = survey(
        place, jnp.array(table, jnp.int32), documents, readers.T, entries, length, window,
        slots, slots * tokens,
    )

    def swap(value, r):
        return lax.ppermute(value, "head", [(h, h ^ r) for h in range(slots)])

    def exchanged(sources, widths, before=()):
        copies = []
        for r in range(slots):
            column = 0
            for source, width in enumerate(widths):
                target, row = (r, 0) if r < 2 else (1 + r // 2, r % 2 * tokens)
                copies.append(
                    (
                        source,
                        0,
                        tokens,
                        lambda h, r=r, width=width: (h ^ r) * width,
                        width,
                        target,
                        row,
                        column,
                    )
                )
                column += width
        shapes = [(tokens, sum(widths))] * 2 + [(2 * tokens, sum(widths))] * (slots // 2 - 1)
        if before:
            pieces = move(place, sources, copies, shapes[: slots // 2 + 1], in_vmem, in_vmem)
        else:
            head = lax.axis_index("head")

            def piece(r):
                return jnp.concatenate(
                    [
                        lax.dynamic_slice_in_dim(source, (head ^ r) * width, width, 1)
                        for source, width in zip(sources, widths)
                    ],
                    axis=1,
                )

            pieces = [piece(r) for r in range(min(2, slots))]
            pieces += [
                jnp.concatenate([piece(r), piece(r + 1)], axis=0) for r in range(2, slots, 2)
            ]
        spots = {0: (pieces[0], 0), 1: (swap(pieces[1], 1), 0)}
        sent = pieces[2:]
        if before and sent:
            sent = lax.optimization_barrier((tuple(sent), *before))[0]
        for r in range(2, slots, 2):
            spots[r] = (swap(sent[r // 2 - 1], r), 0)
        return spots

    def shared(spots, after=()):
        for r in range(2, slots, 2):
            got = spots[r][0]
            if after:
                got = lax.optimization_barrier((got, *after))[0]
            spots[r] = (got, 0)
            spots[r + 1] = (swap(got[tokens:], 1), 0)

    def part_of(spots, group, after=()):
        return move(
            place,
            [spots[r][0] for r in group],
            [
                (
                    number,
                    spots[r][1],
                    tokens,
                    0,
                    2 * local_keys,
                    0,
                    lambda h, r=r: ((h % 2) ^ r) * tokens - group[0] * tokens,
                    0,
                )
                for number, r in enumerate(group)
            ],
            [(len(group) * tokens, 2 * local_keys)],
            in_vmem,
            in_vmem,
            after,
        )[0]

    def send(part, k, after=()):
        pairs, used = [], set()
        for h in range(slots):
            for target, (source, _, slot) in plans[part][h % 2][k].items():
                pairs.append((h * shards + source, h * shards + target))
                used.add(slot)
        if len(used) > 1:
            candidates = {slot: held[part][slot] for slot in used}
            operand = choose(info, 2 + 3 * length + part * length + k, candidates, after)
        else:
            operand = held[part][min(used)]
            if after:
                operand = lax.optimization_barrier((operand, *after))[0]
        held[part][k + 1] = lax.ppermute(operand, ("head", "ctx"), pairs)
        return operand

    def attended(heads, chosen, state, final=None):
        asked = [queries[r] for r in range(slots)]
        plain = [slot[0] if isinstance(slot, tuple) else slot for slot in chosen]
        blocks = [[part[slot] for part in held] for slot in plain]
        return attend(info, doc_rows, asked, heads, blocks, chosen, state, final)

    halves = [range(key_heads)]
    if key_heads % 2 == 0:
        halves = [range(key_heads // 2), range(key_heads // 2, key_heads)]
    later = range(1, len(groups))
    spots = exchanged([key_matrix, value_matrix], [local_keys] * 2)
    held = [{0: part_of(spots, groups[0])}]
    send(0, 0)
    send(0, 1, [info])
    across = range(2, slots, 2)
    queries = exchanged([query_matrix], [local_queries], [spots[r][0] for r in across])
    arrived = [queries[r][0] for r in across]
    shared(spots, [queries[0][0]])
    for part in later:
        held.append({0: part_of(spots, groups[part], [held[0][1], held[0][2]])})
        send(part, 0)
        send(part, 1)
    shared(queries)
    send(0, 2)
    state = attended(range(key_heads), [0], None)
    send(0, 3, arrived)
    more = range(4, length)
    for part in later:
        for k in more:
            send(part, k)
        send(part, 2, [held[part][2], state[1]] + [held[part][k + 1] for k in more])
    state = attended(range(key_heads), [1, (2, 1, False)], state)
    for k in more:
        send(0, k, [state[1]])
    for part in later:
        send(part, 3, [held[0][4], state[1]])
    state = attended(
        range(key_heads), [(2, 1, True), 3] + [k + 1 for k in more], state
    )
    results = []
    others = list(range(1, slots))
    for heads in halves:
        outs = attended(heads, [4], state, others)
        results.append([(swap(out, r), r, heads[0]) for r, out in zip(others, outs)])
    results[0].append((attended(range(key_heads), [4], state, [0])[0], 0, 0))
    whole = ()
    for group in results:
        whole = move(
            place,
            [out for out, _, _ in group],
            [
                (
                    number,
                    0,
                    tokens,
                    0,
                    out.shape[1],
                    0,
                    0,
                    lambda h, r=r, first=first: (h ^ r) * local_queries
                    + first * GROUP * HEAD_WIDTH,
                )
                for number, (out, r, first) in enumerate(group)
            ],
            [query_matrix.shape],
            in_vmem,
            anywhere,
            (),
            whole,
        )
    return whole[0]


def solution(mesh):
    placed = (
        P(("ctx", "head"), None),
        P(("ctx", "head"), None),
        P(("ctx", "head"), None),
        P(),
        P(),
    )
    return jax.shard_map(
        per_device, mesh=mesh, in_specs=placed, out_specs=P(("ctx", "head"), None), check_vma=False
    )
```
